512 devices in a mesh: kz: 64 (over z, y_lo, core), en: 8 (over y_hi, x).
Axes of the slice: x: 4, y: 4 (y_hi: 2, y_lo: 2; y = y_hi * 2 + y_lo), z: 16, core: 2. Of those that a mesh axis runs over, the one named last changes fastest.
Arguments:
- lesser: bfloat16 [64, 16, 1, 256, 512], P('kz', 'en'), may hold values from -6 to 6
- greater: bfloat16 [64, 16, 1, 256, 512], P('kz', 'en'), may hold values from -6 to 6
- coupling: bfloat16 [1, 4, 256, 256], replicated, may hold values from -0.375 to 0.375
- occupation: float32 [4], replicated, may hold values from 0.2 to 3
- offsets: int32 [4], replicated, may hold values from 1 to 2, as said below
- readers: int32 [64, 5], P('kz'), may hold values 0 or 1
- weights: float32 [5], replicated, may hold values from 0.3 to 1
Outputs:
- sigma_lesser: bfloat16 [64, 16, 1, 256, 512], P('kz', 'en')
- sigma_greater: bfloat16 [64, 16, 1, 256, 512], P('kz', 'en')
The draws below stay inside these ranges and needn't reach their ends.
Inputs may be any that keep to these rules, and one draw needn't show every extreme that they name: `offsets`: each branch's phonon energy lies between 1 and 2 grid steps, and some branch has exactly 2.
All inputs are finite; a program needn't handle non-finite values. No bound on the sum of `readers` on one device may be relied on, other than what follows from the above.
Results may differ from the reference program's by a relative error of at most 0.018.
Values may be sent and summed in bfloat16 or wider, within the bound.
No kernel may reach another device: no remote copies, remote signals or barrier semaphores. Data moves between devices by JAX's collectives and lax.ppermute only.
A program may use at most 64 MiB of HBM per device.

```python
import math
import jax
import jax.numpy as jnp
from jax import lax

ORB = 256
SLABS = 1
BRANCHES = 4
REACH = 2
QW = 5
OMAX = 2
ENERGIES = 16
MOMENTA = 64


def draw_offsets(key, part):
    first, second = jax.random.split(key)
    values = jax.random.randint(first, (BRANCHES,), 1, OMAX + 1)
    picked = jax.random.randint(second, (), 0, BRANCHES)
    return jnp.where(jnp.arange(BRANCHES) == picked, OMAX, values).astype(jnp.int32)


def touch_ends(result, key, smallest, high):
    extent = result.shape
    index_at = [jax.random.randint(jax.random.fold_in(key, axis), (), 0, extent[axis]) for axis in range(len(extent))]
    result = result.at[tuple(index_at)].set(smallest)
    longest = extent.index(max(extent))
    index_at[longest] = (index_at[longest] + 1) % extent[longest]
    return result.at[tuple(index_at)].set(high)


def level_of(own_key, shape, pieces, low, high):
    loudness = 1.0
    for axis_at, shards_of in pieces:
        draws = jax.random.uniform(jax.random.fold_in(jax.random.fold_in(own_key, 6), axis_at), (shards_of,), jnp.float32, low / len(pieces), high / len(pieces))
        loudness = loudness * jnp.repeat(jnp.exp(draws), shape[axis_at] // shards_of).reshape((-1,) + (1,) * (len(shape) - 1 - axis_at))
    return loudness


def normal_values(own_key, shape, deviation, limit, cuts=(), held_as=jnp.bfloat16):
    array = jax.random.normal(own_key, shape, jnp.float32) * deviation
    if len(cuts) > 0:
        array = level_of(own_key, shape, cuts, -0.22, 0.18) * array
    return jnp.clip(array, min=-limit, max=limit).astype(held_as)


def setup_inputs(seed: int = 0) -> dict:
    arg_keys = jax.random.split(jax.random.key(seed), 8)
    lesser = normal_values(arg_keys[0], (MOMENTA, ENERGIES, SLABS, ORB, 2 * ORB), 1.0, 6.0, ((0, 64), (1, 8)))
    greater = normal_values(arg_keys[1], (MOMENTA, ENERGIES, SLABS, ORB, 2 * ORB), 1.0, 6.0, ((0, 64), (1, 8)))
    coupling = normal_values(arg_keys[2], (SLABS, BRANCHES, ORB, ORB), ORB ** -0.5, 0.375)
    occupation = jnp.clip(jnp.exp(jax.random.uniform(arg_keys[3], (BRANCHES,), jnp.float32, math.log(0.2), math.log(3.0))), 0.2, 3.0)
    offsets = draw_offsets(jax.random.fold_in(arg_keys[7], 71), 0)
    readers = touch_ends((jax.random.randint(arg_keys[5], (MOMENTA, QW), 0, 4) < 3).astype(jnp.int32), jax.random.fold_in(arg_keys[5], 1), 0, 1)
    weights = jnp.clip(jnp.exp(jax.random.uniform(arg_keys[6], (QW,), jnp.float32, math.log(0.3), math.log(1.0))), 0.3, 1.0)
    return {"lesser": lesser, "greater": greater, "coupling": coupling, "occupation": occupation, "offsets": offsets, "readers": readers, "weights": weights}


def reference(lesser, greater, coupling, occupation, offsets, readers, weights):
    def window(k):
        acc_l = jnp.zeros(lesser.shape[1:], jnp.float32)
        acc_g = jnp.zeros(greater.shape[1:], jnp.float32)
        for j in range(QW):
            src = (k - (j - REACH)) % MOMENTA
            coef = weights[j] * readers[k, j].astype(jnp.float32)
            acc_l = acc_l + coef * lesser[src].astype(jnp.float32)
            acc_g = acc_g + coef * greater[src].astype(jnp.float32)
        return acc_l.astype(jnp.bfloat16), acc_g.astype(jnp.bfloat16)

    win_l, win_g = lax.map(window, jnp.arange(MOMENTA, dtype=jnp.int32))

    def energy_pass(pair):
        blocks_l, blocks_g = pair
        pad_width = ((OMAX, OMAX), (0, 0), (0, 0), (0, 0))
        ext_l = jnp.pad(blocks_l.astype(jnp.float32), pad_width)
        ext_g = jnp.pad(blocks_g.astype(jnp.float32), pad_width)
        total_l = jnp.zeros((ENERGIES, SLABS, ORB, 2, ORB), jnp.float32)
        total_g = jnp.zeros((ENERGIES, SLABS, ORB, 2, ORB), jnp.float32)
        for branch in range(BRANCHES):
            shift = offsets[branch].astype(jnp.int32)
            occ = occupation[branch]
            up_l = lax.dynamic_slice_in_dim(ext_l, OMAX + shift, ENERGIES, 0)
            down_l = lax.dynamic_slice_in_dim(ext_l, OMAX - shift, ENERGIES, 0)
            up_g = lax.dynamic_slice_in_dim(ext_g, OMAX + shift, ENERGIES, 0)
            down_g = lax.dynamic_slice_in_dim(ext_g, OMAX - shift, ENERGIES, 0)
            mix_l = ((occ + 1.0) * up_l + occ * down_l).astype(jnp.bfloat16).astype(jnp.float32)
            mix_g = (occ * up_g + (occ + 1.0) * down_g).astype(jnp.bfloat16).astype(jnp.float32)
            mat = coupling[:, branch].astype(jnp.float32)
            for mix, name in ((mix_l, 0), (mix_g, 1)):
                left = jnp.einsum("sij,esjc->esic", mat, mix).astype(jnp.bfloat16).astype(jnp.float32)
                left = left.reshape(ENERGIES, SLABS, ORB, 2, ORB)
                right = jnp.einsum("esirc,sjc->esirj", left, mat)
                if name == 0:
                    total_l = total_l + right
                else:
                    total_g = total_g + right
        shape = (ENERGIES, SLABS, ORB, 2 * ORB)
        return total_l.reshape(shape).astype(jnp.bfloat16), total_g.reshape(shape).astype(jnp.bfloat16)

    sigma_lesser, sigma_greater = lax.map(energy_pass, (win_l, win_g))
    return sigma_lesser, sigma_greater
```

```python
import jax
import jax.numpy as jnp
from jax import lax
from jax.experimental import pallas as pl
from jax.experimental.pallas import tpu as pltpu
from jax.sharding import PartitionSpec as P

BRANCHES = 4
ORB = 256
F32 = jnp.float32
BF16 = jnp.bfloat16


def swap_route(count, bit):
    return [(k, k ^ bit) for k in range(count)]


def plane_route(count, sign):
    return [(k, (k + (sign if (k >> 1) % 2 == 0 else -sign) * 4) % count) for k in range(count)]


def mix(terms):
    acc = terms[0][0] * terms[0][1].astype(F32)
    for factor, block in terms[1:]:
        acc = acc + factor * block.astype(F32)
    return acc.astype(BF16)


def sigma_kernel(occ_ref, off_ref, own_ref, above_ref, below_ref, mat_ref, tra_ref, out_ref, acc_ref, *, plus_up):
    for branch in range(BRANCHES):
        n = occ_ref[branch]
        one = off_ref[branch] == 1
        up_factor = n + 1.0 if plus_up else n
        down_factor = n if plus_up else n + 1.0
        c = mat_ref[branch]
        t = tra_ref[branch]
        for e in range(2):
            if e == 0:
                upper = jnp.where(one, own_ref[1], above_ref[0])
                lower = jnp.where(one, below_ref[1], below_ref[0])
            else:
                upper = jnp.where(one, above_ref[0], above_ref[1])
                lower = jnp.where(one, own_ref[0], below_ref[1])
            mixed = (up_factor * upper.astype(F32) + down_factor * lower.astype(F32)).astype(BF16)
            left = jnp.dot(c, mixed, preferred_element_type=F32).astype(BF16)
            for h in range(2):
                cols = slice(h * ORB, (h + 1) * ORB)
                right = jnp.dot(left[:, cols], t, preferred_element_type=F32)
                if branch == 0:
                    acc_ref[e, :, cols] = right
                elif branch < BRANCHES - 1:
                    acc_ref[e, :, cols] += right
                else:
                    out_ref[e, :, cols] = (acc_ref[e, :, cols] + right).astype(BF16)


def sigma(own, above, below, mats, trans, occupation, offsets, plus_up):
    import functools

    vmem = pl.BlockSpec(memory_space=pltpu.VMEM)
    smem = pl.BlockSpec(memory_space=pltpu.SMEM)
    return pl.pallas_call(
        functools.partial(sigma_kernel, plus_up=plus_up),
        out_shape=jax.ShapeDtypeStruct(own.shape, BF16),
        in_specs=[smem, smem, vmem, vmem, vmem, vmem, vmem],
        out_specs=vmem,
        scratch_shapes=[pltpu.VMEM(own.shape, F32)],
        compiler_params=pltpu.CompilerParams(vmem_limit_bytes=24 * 1024 * 1024),
        cost_estimate=pl.CostEstimate(flops=2**30, bytes_accessed=3 * 2**20, transcendentals=0),
    )(occupation, offsets, own, above, below, mats, trans)


def local(lesser, greater, coupling, occupation, offsets, readers, weights):
    count = lax.axis_size("kz")
    energies = lax.axis_size("en")
    k = lax.axis_index("kz")
    core1 = (k & 1) == 1
    odd = ((k >> 1) & 1) == 1
    up = [(i, i + 1) for i in range(energies - 1)]
    down = [(i + 1, i) for i in range(energies - 1)]

    def kz(block, route):
        return lax.ppermute(block, "kz", route)

    shape = (2, ORB, 2 * ORB)
    xl = lesser.reshape(shape)
    xg = greater.reshape(shape)
    mats = coupling[0]
    trans = jnp.swapaxes(mats, 1, 2)
    f = weights * readers[0].astype(F32)
    fc = kz(f, swap_route(count, 1))
    fy = kz(f, swap_route(count, 2))

    yl = kz(xl, swap_route(count, 2))
    zg = kz(xg, plane_route(count, -1))
    cg = kz(xg, swap_route(count, 1))
    zl = kz(yl, plane_route(count, 1))
    czg = kz(zg, swap_route(count, 1))
    zero = jnp.zeros((), F32)
    pg = mix([
        (jnp.where(odd, fy[0], fy[4]), xg),
        (jnp.where(odd, fy[4], fy[0]), zg),
        (jnp.where(odd, jnp.where(core1, fy[1], zero), jnp.where(core1, zero, fy[3])), cg),
        (jnp.where(odd, jnp.where(core1, zero, fy[3]), jnp.where(core1, fy[1], zero)), czg),
    ])
    rg = kz(pg, swap_route(count, 2))
    wg = mix([(f[2], xg), (jnp.where(core1, f[3], f[1]), cg), (jnp.ones((), F32), rg)])
    far = jnp.where(core1, fc[3], fc[1])
    ql = mix([
        (jnp.where(core1, fc[1], fc[3]), xl),
        (jnp.where(odd == core1, far, zero), yl),
        (jnp.where(odd == core1, zero, far), zl),
    ])
    rl = kz(ql, swap_route(count, 1))
    wl = mix([
        (f[2], xl),
        (jnp.where(odd, f[4], f[0]), yl),
        (jnp.where(odd, f[0], f[4]), zl),
        (jnp.ones((), F32), rl),
    ])

    def en(block):
        below = lax.ppermute(block, "en", up)
        above = lax.ppermute(block, "en", down)
        return above, below

    al, bl = en(wl)
    ag, bg = en(wg)
    sl = sigma(wl, al, bl, mats, trans, occupation, offsets, True)
    sg = sigma(wg, ag, bg, mats, trans, occupation, offsets, False)
    return sl.reshape(lesser.shape), sg.reshape(greater.shape)


def solution(mesh):
    wide = P("kz", "en", None, None, None)
    return jax.shard_map(
        local,
        mesh=mesh,
        in_specs=(wide, wide, P(), P(), P(), P("kz", None), P()),
        out_specs=(wide, wide),
        check_vma=False,
    )
```

```python
import functools

import jax
import jax.numpy as jnp
from jax import lax
from jax.experimental import pallas as pl
from jax.experimental.pallas import tpu as pltpu
from jax.sharding import PartitionSpec as P

BRANCHES = 4
ORB = 256
SHAPE = (2, ORB, 2 * ORB)
ROWS = 32
F32 = jnp.float32
BF16 = jnp.bfloat16
VMEM = pl.BlockSpec(memory_space=pltpu.VMEM)
SMEM = pl.BlockSpec(memory_space=pltpu.SMEM)
PARAMS = pltpu.CompilerParams(vmem_limit_bytes=24 * 1024 * 1024)


def swap_route(count, bit):
    return [(k, k ^ bit) for k in range(count)]


def plane_route(count, sign):
    return [(k, (k + (sign if (k >> 1) % 2 == 0 else -sign) * 4) % count) for k in range(count)]


def pair_route(count, first):
    pairs = [(i, i + 1) for i in range(first, count - 1, 2)]
    return pairs + [(j, i) for i, j in pairs]


def weighted(factors, refs, out_ref):
    for e in range(2):
        for r in range(0, ORB, ROWS):
            rows = slice(r, r + ROWS)
            acc = None
            for factor, ref in zip(factors, refs):
                term = ref[e, rows, :].astype(F32)
                if factor is not None:
                    term = factor * term
                acc = term if acc is None else acc + term
            out_ref[e, rows, :] = acc.astype(BF16)


def pair_partial_kernel(pos_ref, f_ref, x_ref, z_ref, c_ref, cz_ref, out_ref):
    core1, odd = pos_ref[0] == 1, pos_ref[1] == 1
    two = jnp.where(odd, f_ref[0], f_ref[4])
    far = jnp.where(odd, f_ref[4], f_ref[0])
    side = jnp.where(core1, f_ref[1], f_ref[3])
    own_side = core1 == odd
    fc = jnp.where(own_side, side, 0.0)
    fz = jnp.where(own_side, 0.0, side)
    weighted((two, far, fc, fz), (x_ref, z_ref, c_ref, cz_ref), out_ref)


def core_partial_kernel(pos_ref, f_ref, x_ref, y_ref, z_ref, out_ref):
    core1, odd = pos_ref[0] == 1, pos_ref[1] == 1
    near = jnp.where(core1, f_ref[1], f_ref[3])
    far = jnp.where(core1, f_ref[3], f_ref[1])
    by_pair = core1 == odd
    weighted((near, jnp.where(by_pair, far, 0.0), jnp.where(by_pair, 0.0, far)), (x_ref, y_ref, z_ref), out_ref)


def lesser_window_kernel(pos_ref, f_ref, x_ref, y_ref, z_ref, r_ref, out_ref):
    odd = pos_ref[1] == 1
    fy = jnp.where(odd, f_ref[4], f_ref[0])
    fz = jnp.where(odd, f_ref[0], f_ref[4])
    weighted((f_ref[2], fy, fz, None), (x_ref, y_ref, z_ref, r_ref), out_ref)


def greater_window_kernel(pos_ref, f_ref, x_ref, c_ref, r_ref, out_ref):
    core1 = pos_ref[0] == 1
    weighted((f_ref[2], jnp.where(core1, f_ref[3], f_ref[1]), None), (x_ref, c_ref, r_ref), out_ref)


def combine(kernel, pos, factors, *blocks):
    return pl.pallas_call(
        kernel,
        out_shape=jax.ShapeDtypeStruct(SHAPE, BF16),
        in_specs=[SMEM, SMEM] + [VMEM] * len(blocks),
        out_specs=VMEM,
        compiler_params=PARAMS,
        cost_estimate=pl.CostEstimate(flops=2**21, bytes_accessed=2**21, transcendentals=0),
    )(pos, factors, *blocks)


def sigma_kernel(pos_ref, occ_ref, off_ref, own_ref, a_ref, b_ref, mat_ref, tra_ref, out_ref, ext_ref, acc_ref, *, plus_up):
    swap = pos_ref[2] == 1

    @pl.when(swap)
    def _():
        ext_ref[0:2] = b_ref[...]
        ext_ref[4:6] = a_ref[...]

    @pl.when(jnp.logical_not(swap))
    def _():
        ext_ref[0:2] = a_ref[...]
        ext_ref[4:6] = b_ref[...]

    ext_ref[2:4] = own_ref[...]
    for branch in range(BRANCHES):
        n = occ_ref[branch]
        shift = off_ref[branch]
        up_factor = n + 1.0 if plus_up else n
        down_factor = n if plus_up else n + 1.0
        c = mat_ref[branch]
        t = tra_ref[branch]
        for e in range(2):
            upper = ext_ref[2 + e + shift].astype(F32)
            lower = ext_ref[2 + e - shift].astype(F32)
            mixed = (up_factor * upper + down_factor * lower).astype(BF16)
            left = jnp.dot(c, mixed, preferred_element_type=F32).astype(BF16)
            for h in range(2):
                cols = slice(h * ORB, (h + 1) * ORB)
                right = jnp.dot(left[:, cols], t, preferred_element_type=F32)
                if branch == 0:
                    acc_ref[e, :, cols] = right
                elif branch < BRANCHES - 1:
                    acc_ref[e, :, cols] += right
                else:
                    out_ref[e, :, cols] = (acc_ref[e, :, cols] + right).astype(BF16)


def sigma(pos, occupation, offsets, own, a, b, mats, trans, plus_up):
    return pl.pallas_call(
        functools.partial(sigma_kernel, plus_up=plus_up),
        out_shape=jax.ShapeDtypeStruct(SHAPE, BF16),
        in_specs=[SMEM] * 3 + [VMEM] * 5,
        out_specs=VMEM,
        scratch_shapes=[pltpu.VMEM((6, ORB, 2 * ORB), BF16), pltpu.VMEM(SHAPE, F32)],
        compiler_params=PARAMS,
        cost_estimate=pl.CostEstimate(flops=2**30, bytes_accessed=3 * 2**20, transcendentals=0),
    )(pos, occupation, offsets, own, a, b, mats, trans)


def local(lesser, greater, coupling, occupation, offsets, readers, weights):
    count = lax.axis_size("kz")
    energies = lax.axis_size("en")
    k = lax.axis_index("kz")
    pos = jnp.stack((k & 1, (k >> 1) & 1, lax.axis_index("en") & 1)).astype(jnp.int32)

    def kz(block, route):
        return lax.ppermute(block, "kz", route)

    xl = lesser.reshape(SHAPE)
    xg = greater.reshape(SHAPE)
    mats = coupling[0]
    trans = jnp.swapaxes(mats, 1, 2)
    f = weights * readers[0].astype(F32)

    yl = kz(xl, swap_route(count, 2))
    zg = kz(xg, plane_route(count, -1))
    cg = kz(xg, swap_route(count, 1))
    fy = kz(f, swap_route(count, 2))
    fc = kz(f, swap_route(count, 1))
    yl, f, fy, fc, pos, trans = lax.optimization_barrier((yl, f, fy, fc, pos, trans))
    zl = kz(yl, plane_route(count, 1))
    czg = kz(zg, swap_route(count, 1))
    pg = combine(pair_partial_kernel, pos, fy, xg, zg, cg, czg)
    rg = kz(pg, swap_route(count, 2))
    zl, _ = lax.optimization_barrier((zl, pg))
    ql = combine(core_partial_kernel, pos, fc, xl, yl, zl)
    rl = kz(ql, swap_route(count, 1))
    wl = combine(lesser_window_kernel, pos, f, xl, yl, zl, rl)
    wg = combine(greater_window_kernel, pos, f, xg, cg, rg)

    odd_pairs, even_pairs = pair_route(energies, 1), pair_route(energies, 0)
    bl = lax.ppermute(wl, "en", even_pairs)
    al = lax.ppermute(wl, "en", odd_pairs)
    bg = lax.ppermute(wg, "en", even_pairs)
    ag = lax.ppermute(wg, "en", odd_pairs)
    sl = sigma(pos, occupation, offsets, wl, al, bl, mats, trans, True)
    sg = sigma(pos, occupation, offsets, wg, ag, bg, mats, trans, False)
    return sl.reshape(lesser.shape), sg.reshape(greater.shape)


def solution(mesh):
    wide = P("kz", "en", None, None, None)
    return jax.shard_map(
        local,
        mesh=mesh,
        in_specs=(wide, wide, P(), P(), P(), P("kz", None), P()),
        out_specs=(wide, wide),
        check_vma=False,
    )
```

```python
import functools

import jax
import jax.numpy as jnp
from jax import lax
from jax.experimental import pallas as pl
from jax.experimental.pallas import tpu as pltpu
from jax.sharding import PartitionSpec as P

BRANCHES = 4
ORB = 256
SHAPE = (2, ORB, 2 * ORB)
ROWS = 32
F32 = jnp.float32
BF16 = jnp.bfloat16
VMEM = pl.BlockSpec(memory_space=pltpu.VMEM)
SMEM = pl.BlockSpec(memory_space=pltpu.SMEM)
PARAMS = pltpu.CompilerParams(vmem_limit_bytes=24 * 1024 * 1024)


def swap_route(count, bit):
    return [(k, k ^ bit) for k in range(count)]


def plane_route(count, sign):
    return [(k, (k + (sign if (k >> 1) % 2 == 0 else -sign) * 4) % count) for k in range(count)]


def pair_route(count, first):
    pairs = [(i, i + 1) for i in range(first, count - 1, 2)]
    return pairs + [(j, i) for i, j in pairs]


def weighted(factors, refs, out_ref):
    for e in range(2):
        for r in range(0, ORB, ROWS):
            rows = slice(r, r + ROWS)
            acc = None
            for factor, ref in zip(factors, refs):
                term = ref[e, rows, :].astype(F32)
                if factor is not None:
                    term = factor * term
                acc = term if acc is None else acc + term
            out_ref[e, rows, :] = acc.astype(BF16)


def pair_partial_kernel(pos_ref, f_ref, x_ref, z_ref, c_ref, cz_ref, out_ref):
    core1, odd = pos_ref[0] == 1, pos_ref[1] == 1
    two = jnp.where(odd, f_ref[0], f_ref[4])
    far = jnp.where(odd, f_ref[4], f_ref[0])
    side = jnp.where(core1, f_ref[1], f_ref[3])
    own_side = core1 == odd
    fc = jnp.where(own_side, side, 0.0)
    fz = jnp.where(own_side, 0.0, side)
    weighted((two, far, fc, fz), (x_ref, z_ref, c_ref, cz_ref), out_ref)


def core_partial_kernel(pos_ref, f_ref, x_ref, y_ref, z_ref, out_ref):
    core1, odd = pos_ref[0] == 1, pos_ref[1] == 1
    near = jnp.where(core1, f_ref[1], f_ref[3])
    far = jnp.where(core1, f_ref[3], f_ref[1])
    by_pair = core1 == odd
    weighted((near, jnp.where(by_pair, far, 0.0), jnp.where(by_pair, 0.0, far)), (x_ref, y_ref, z_ref), out_ref)


def greater_window_kernel(pos_ref, f_ref, x_ref, c_ref, r_ref, out_ref):
    core1 = pos_ref[0] == 1
    weighted((f_ref[2], jnp.where(core1, f_ref[3], f_ref[1]), None), (x_ref, c_ref, r_ref), out_ref)


def lesser_window_kernel(pos_ref, f_ref, x_ref, y_ref, z_ref, r_ref, out_ref):
    odd = pos_ref[1] == 1
    fy = jnp.where(odd, f_ref[4], f_ref[0])
    fz = jnp.where(odd, f_ref[0], f_ref[4])
    weighted((f_ref[2], fy, fz, None), (x_ref, y_ref, z_ref, r_ref), out_ref)


def combine(kernel, pos, factors, *blocks):
    return pl.pallas_call(
        kernel,
        out_shape=jax.ShapeDtypeStruct(SHAPE, BF16),
        in_specs=[SMEM, SMEM] + [VMEM] * len(blocks),
        out_specs=VMEM,
        compiler_params=PARAMS,
        cost_estimate=pl.CostEstimate(flops=2**21, bytes_accessed=2**21, transcendentals=0),
    )(pos, factors, *blocks)


def stage_kernel(a_ref, b_ref, c_ref, d_ref):
    c_ref[...] = a_ref[...]
    d_ref[...] = b_ref[...]


def stage(a, b):
    shape = jax.ShapeDtypeStruct(SHAPE, BF16)
    return pl.pallas_call(
        stage_kernel, out_shape=[shape, shape], in_specs=[VMEM, VMEM], out_specs=[VMEM, VMEM], compiler_params=PARAMS
    )(a, b)


def sigma_part(occ_ref, off_ref, own_ref, below_ref, above_ref, mat_ref, e, cols, plus_up):
    acc = None
    for branch in range(BRANCHES):
        n = occ_ref[branch]
        one = off_ref[branch] == 1
        up_factor = n + 1.0 if plus_up else n
        down_factor = n if plus_up else n + 1.0
        if e == 0:
            upper = jnp.where(one, own_ref[1, :, cols], above_ref[0, :, cols])
            lower = jnp.where(one, below_ref[1, :, cols], below_ref[0, :, cols])
        else:
            upper = jnp.where(one, above_ref[0, :, cols], above_ref[1, :, cols])
            lower = jnp.where(one, own_ref[0, :, cols], below_ref[1, :, cols])
        mixed = (up_factor * upper.astype(F32) + down_factor * lower.astype(F32)).astype(BF16)
        left = jnp.dot(mat_ref[branch], mixed, preferred_element_type=F32).astype(BF16)
        right = lax.dot_general(left, mat_ref[branch], (((1,), (1,)), ((), ())), preferred_element_type=F32)
        acc = right if acc is None else acc + right
    return acc.astype(BF16)


def by_parity(pos_ref, a_ref, b_ref, body):
    swap = pos_ref[2] == 1
    pl.when(swap)(lambda: body(b_ref, a_ref))
    pl.when(jnp.logical_not(swap))(lambda: body(a_ref, b_ref))


def sigma_kernel(pos_ref, occ_ref, off_ref, own_ref, b_ref, a_ref, mat_ref, out_ref, *, plus_up):
    def body(below_ref, above_ref):
        for e in range(2):
            for h in range(2):
                cols = slice(h * ORB, (h + 1) * ORB)
                out_ref[e, :, cols] = sigma_part(
                    occ_ref, off_ref, own_ref, below_ref, above_ref, mat_ref, e, cols, plus_up
                )

    by_parity(pos_ref, a_ref, b_ref, body)


def sigma(plus_up, pos, occupation, offsets, *blocks):
    return pl.pallas_call(
        functools.partial(sigma_kernel, plus_up=plus_up),
        out_shape=jax.ShapeDtypeStruct(SHAPE, BF16),
        in_specs=[SMEM] * 3 + [VMEM] * len(blocks),
        out_specs=VMEM,
        compiler_params=PARAMS,
        cost_estimate=pl.CostEstimate(flops=2**30, bytes_accessed=3 * 2**20, transcendentals=0),
    )(pos, occupation, offsets, *blocks)


def local(lesser, greater, coupling, occupation, offsets, readers, weights):
    count = lax.axis_size("kz")
    energies = lax.axis_size("en")
    k = lax.axis_index("kz")
    pos = jnp.stack((k & 1, (k >> 1) & 1, lax.axis_index("en") & 1)).astype(jnp.int32)

    def kz(block, route):
        return lax.ppermute(block, "kz", route)

    xl = lesser.reshape(SHAPE)
    xg = greater.reshape(SHAPE)
    mats = coupling[0]
    xlv, xgv = stage(xl, xg)
    f = weights * readers[0].astype(F32)

    yl = kz(xl, swap_route(count, 2))
    zg = kz(xg, plane_route(count, -1))
    cg = kz(xg, swap_route(count, 1))
    fy = kz(f, swap_route(count, 2))
    yl, f, fy, pos, xlv, xgv = lax.optimization_barrier((yl, f, fy, pos, xlv, xgv))
    zl = kz(yl, plane_route(count, 1))
    czg = kz(zg, swap_route(count, 1))
    pg = combine(pair_partial_kernel, pos, fy, xgv, zg, cg, czg)
    rg = kz(pg, swap_route(count, 2))
    late, _ = lax.optimization_barrier((f, pg))
    fc = kz(late, swap_route(count, 1))
    zl, fc = lax.optimization_barrier((zl, fc))
    ql = combine(core_partial_kernel, pos, fc, xlv, yl, zl)
    rl = kz(ql, swap_route(count, 1))
    wg = combine(greater_window_kernel, pos, f, xgv, cg, rg)
    wl = combine(lesser_window_kernel, pos, f, xlv, yl, zl, rl)

    odd_pairs, even_pairs = pair_route(energies, 1), pair_route(energies, 0)
    bl = lax.ppermute(wl, "en", even_pairs)
    al = lax.ppermute(wl, "en", odd_pairs)
    bg = lax.ppermute(wg, "en", even_pairs)
    ag = lax.ppermute(wg, "en", odd_pairs)
    sl = sigma(True, pos, occupation, offsets, wl, bl, al, mats)
    sg = sigma(False, pos, occupation, offsets, wg, bg, ag, mats)
    return sl.reshape(lesser.shape), sg.reshape(greater.shape)


def solution(mesh):
    wide = P("kz", "en", None, None, None)
    return jax.shard_map(
        local,
        mesh=mesh,
        in_specs=(wide, wide, P(), P(), P(), P("kz", None), P()),
        out_specs=(wide, wide),
        check_vma=False,
    )
```

```python
import functools

import jax
import jax.numpy as jnp
from jax import lax
from jax.experimental import pallas as pl
from jax.experimental.pallas import tpu as pltpu
from jax.sharding import PartitionSpec as P

BRANCHES = 4
ORB = 256
SHAPE = (2, ORB, 2 * ORB)
ROWS = 32
F32 = jnp.float32
BF16 = jnp.bfloat16
VMEM = pl.BlockSpec(memory_space=pltpu.VMEM)
SMEM = pl.BlockSpec(memory_space=pltpu.SMEM)
PARAMS = pltpu.CompilerParams(vmem_limit_bytes=24 * 1024 * 1024)


def swap_route(count, bit):
    return [(k, k ^ bit) for k in range(count)]


def plane_route(count, sign):
    return [(k, (k + (sign if (k >> 1) % 2 == 0 else -sign) * 4) % count) for k in range(count)]


def pair_route(count, first):
    pairs = [(i, i + 1) for i in range(first, count - 1, 2)]
    return pairs + [(j, i) for i, j in pairs]


def weighted(factors, refs, out_ref):
    for e in range(2):
        for r in range(0, ORB, ROWS):
            rows = slice(r, r + ROWS)
            acc = None
            for factor, ref in zip(factors, refs):
                term = ref[e, rows, :].astype(F32)
                if factor is not None:
                    term = factor * term
                acc = term if acc is None else acc + term
            out_ref[e, rows, :] = acc.astype(BF16)


def pair_partial_kernel(pos_ref, f_ref, x_ref, z_ref, c_ref, cz_ref, out_ref):
    core1, odd = pos_ref[0] == 1, pos_ref[1] == 1
    two = jnp.where(odd, f_ref[0], f_ref[4])
    far = jnp.where(odd, f_ref[4], f_ref[0])
    side = jnp.where(core1, f_ref[1], f_ref[3])
    own_side = core1 == odd
    fc = jnp.where(own_side, side, 0.0)
    fz = jnp.where(own_side, 0.0, side)
    weighted((two, far, fc, fz), (x_ref, z_ref, c_ref, cz_ref), out_ref)


def core_partial_kernel(pos_ref, f_ref, x_ref, y_ref, z_ref, out_ref):
    core1, odd = pos_ref[0] == 1, pos_ref[1] == 1
    near = jnp.where(core1, f_ref[1], f_ref[3])
    far = jnp.where(core1, f_ref[3], f_ref[1])
    by_pair = core1 == odd
    weighted((near, jnp.where(by_pair, far, 0.0), jnp.where(by_pair, 0.0, far)), (x_ref, y_ref, z_ref), out_ref)


def greater_window_kernel(pos_ref, f_ref, x_ref, c_ref, r_ref, out_ref):
    core1 = pos_ref[0] == 1
    weighted((f_ref[2], jnp.where(core1, f_ref[3], f_ref[1]), None), (x_ref, c_ref, r_ref), out_ref)


def lesser_window_kernel(pos_ref, f_ref, w_ref, x_ref, y_ref, z_ref, r_ref, first_ref, last_ref):
    odd = pos_ref[1] == 1
    f = f_ref[2]
    fy = jnp.where(odd, f_ref[4], f_ref[0])
    fz = jnp.where(odd, f_ref[0], f_ref[4])
    for e in range(2):
        for r in range(0, ORB, ROWS):
            rows = slice(r, r + ROWS)
            first_ref[e, rows, : 2 * ORB] = w_ref[e, rows, :]
            w = (
                f * x_ref[e, rows, :].astype(F32)
                + fy * y_ref[e, rows, :].astype(F32)
                + fz * z_ref[e, rows, :].astype(F32)
                + r_ref[e, rows, :].astype(F32)
            ).astype(BF16)
            first_ref[e, rows, 2 * ORB :] = w[:, :ORB]
            last_ref[e, rows, :] = w[:, ORB:]


def combine(kernel, pos, factors, *blocks, widths=None):
    single = widths is None
    shapes = [jax.ShapeDtypeStruct((2, ORB, w), BF16) for w in (widths or (2 * ORB,))]
    return pl.pallas_call(
        kernel,
        out_shape=shapes[0] if single else shapes,
        in_specs=[SMEM, SMEM] + [VMEM] * len(blocks),
        out_specs=VMEM if single else [VMEM] * len(shapes),
        compiler_params=PARAMS,
        cost_estimate=pl.CostEstimate(flops=2**21, bytes_accessed=2**21, transcendentals=0),
    )(pos, factors, *blocks)


def stage_kernel(a_ref, b_ref, c_ref, d_ref):
    c_ref[...] = a_ref[...]
    d_ref[...] = b_ref[...]


def stage(a, b):
    shape = jax.ShapeDtypeStruct(SHAPE, BF16)
    return pl.pallas_call(
        stage_kernel, out_shape=[shape, shape], in_specs=[VMEM, VMEM], out_specs=[VMEM, VMEM], compiler_params=PARAMS
    )(a, b)


def sigma_part(occ_ref, off_ref, own_ref, below_ref, above_ref, mat_ref, e, cols, plus_up):
    acc = None
    for branch in range(BRANCHES):
        n = occ_ref[branch]
        one = off_ref[branch] == 1
        up_factor = n + 1.0 if plus_up else n
        down_factor = n if plus_up else n + 1.0
        if e == 0:
            upper = jnp.where(one, own_ref[1, :, cols], above_ref[0, :, cols])
            lower = jnp.where(one, below_ref[1, :, cols], below_ref[0, :, cols])
        else:
            upper = jnp.where(one, above_ref[0, :, cols], above_ref[1, :, cols])
            lower = jnp.where(one, own_ref[0, :, cols], below_ref[1, :, cols])
        mixed = (up_factor * upper.astype(F32) + down_factor * lower.astype(F32)).astype(BF16)
        left = jnp.dot(mat_ref[branch], mixed, preferred_element_type=F32).astype(BF16)
        right = lax.dot_general(left, mat_ref[branch], (((1,), (1,)), ((), ())), preferred_element_type=F32)
        acc = right if acc is None else acc + right
    return acc.astype(BF16)


def by_parity(pos_ref, a_ref, b_ref, body):
    swap = pos_ref[2] == 1
    pl.when(swap)(lambda: body(b_ref, a_ref))
    pl.when(jnp.logical_not(swap))(lambda: body(a_ref, b_ref))


def first_sigma_kernel(pos_ref, occ_ref, off_ref, own_ref, b_ref, a_ref, mat_ref, greater_ref, real_ref):
    def body(below_ref, above_ref):
        for e in range(2):
            for h in range(3):
                cols = slice(h * ORB, (h + 1) * ORB)
                part = sigma_part(occ_ref, off_ref, own_ref, below_ref, above_ref, mat_ref, e, cols, h == 2)
                if h < 2:
                    greater_ref[e, :, cols] = part
                else:
                    real_ref[e] = part

    by_parity(pos_ref, a_ref, b_ref, body)


def last_sigma_kernel(pos_ref, occ_ref, off_ref, own_ref, b_ref, a_ref, mat_ref, real_ref, lesser_ref):
    lesser_ref[:, :, :ORB] = real_ref[...]

    def body(below_ref, above_ref):
        for e in range(2):
            part = sigma_part(occ_ref, off_ref, own_ref, below_ref, above_ref, mat_ref, e, slice(0, ORB), True)
            lesser_ref[e, :, ORB:] = part

    by_parity(pos_ref, a_ref, b_ref, body)


def sigma(kernel, widths, pos, occupation, offsets, *blocks):
    return pl.pallas_call(
        kernel,
        out_shape=[jax.ShapeDtypeStruct((2, ORB, w), BF16) for w in widths],
        in_specs=[SMEM] * 3 + [VMEM] * len(blocks),
        out_specs=[VMEM] * len(widths),
        compiler_params=PARAMS,
        cost_estimate=pl.CostEstimate(flops=2**30, bytes_accessed=3 * 2**20, transcendentals=0),
    )(pos, occupation, offsets, *blocks)


def local(lesser, greater, coupling, occupation, offsets, readers, weights):
    count = lax.axis_size("kz")
    energies = lax.axis_size("en")
    k = lax.axis_index("kz")
    pos = jnp.stack((k & 1, (k >> 1) & 1, lax.axis_index("en") & 1)).astype(jnp.int32)

    def kz(block, route):
        return lax.ppermute(block, "kz", route)

    xl = lesser.reshape(SHAPE)
    xg = greater.reshape(SHAPE)
    mats = coupling[0]
    xlv, xgv = stage(xl, xg)
    f = weights * readers[0].astype(F32)

    yl = kz(xl, swap_route(count, 2))
    zg = kz(xg, plane_route(count, -1))
    cg = kz(xg, swap_route(count, 1))
    fy = kz(f, swap_route(count, 2))
    yl, f, fy, pos, xlv, xgv = lax.optimization_barrier((yl, f, fy, pos, xlv, xgv))
    zl = kz(yl, plane_route(count, 1))
    czg = kz(zg, swap_route(count, 1))
    pg = combine(pair_partial_kernel, pos, fy, xgv, zg, cg, czg)
    rg = kz(pg, swap_route(count, 2))
    late, _ = lax.optimization_barrier((f, pg))
    fc = kz(late, swap_route(count, 1))
    zl, fc = lax.optimization_barrier((zl, fc))
    ql = combine(core_partial_kernel, pos, fc, xlv, yl, zl)
    rl = kz(ql, swap_route(count, 1))
    wg = combine(greater_window_kernel, pos, f, xgv, cg, rg)
    w1, w2 = combine(lesser_window_kernel, pos, f, wg, xlv, yl, zl, rl, widths=(3 * ORB, ORB))

    odd_pairs, even_pairs = pair_route(energies, 1), pair_route(energies, 0)
    b1 = lax.ppermute(w1, "en", even_pairs)
    a1 = lax.ppermute(w1, "en", odd_pairs)
    a2 = lax.ppermute(w2, "en", odd_pairs)
    b2 = lax.ppermute(w2, "en", even_pairs)
    sg, real = sigma(first_sigma_kernel, (2 * ORB, ORB), pos, occupation, offsets, w1, b1, a1, mats)
    a2, b2, sg, real = lax.optimization_barrier((a2, b2, sg, real))
    (sl,) = sigma(last_sigma_kernel, (2 * ORB,), pos, occupation, offsets, w2, b2, a2, mats, real)
    return sl.reshape(lesser.shape), sg.reshape(greater.shape)


def solution(mesh):
    wide = P("kz", "en", None, None, None)
    return jax.shard_map(
        local,
        mesh=mesh,
        in_specs=(wide, wide, P(), P(), P(), P("kz", None), P()),
        out_specs=(wide, wide),
        check_vma=False,
    )
```

```python
import functools

import jax
import jax.numpy as jnp
from jax import lax
from jax.experimental import pallas as pl
from jax.experimental.pallas import tpu as pltpu
from jax.sharding import PartitionSpec as P

BRANCHES = 4
ORB = 256
SHAPE = (2, ORB, 2 * ORB)
ROWS = 32
F32 = jnp.float32
BF16 = jnp.bfloat16
VMEM = pl.BlockSpec(memory_space=pltpu.VMEM)
SMEM = pl.BlockSpec(memory_space=pltpu.SMEM)
PARAMS = pltpu.CompilerParams(vmem_limit_bytes=24 * 1024 * 1024)


def swap_route(count, bit):
    return [(k, k ^ bit) for k in range(count)]


def plane_route(count, sign):
    return [(k, (k + (sign if (k >> 1) % 2 == 0 else -sign) * 4) % count) for k in range(count)]


def pair_route(count, first):
    pairs = [(i, i + 1) for i in range(first, count - 1, 2)]
    return pairs + [(j, i) for i, j in pairs]


def weighted(factors, refs, out_ref):
    for e in range(2):
        for r in range(0, ORB, ROWS):
            rows = slice(r, r + ROWS)
            acc = None
            for factor, ref in zip(factors, refs):
                term = ref[e, rows, :].astype(F32)
                if factor is not None:
                    term = factor * term
                acc = term if acc is None else acc + term
            out_ref[e, rows, :] = acc.astype(BF16)


def pair_partial_kernel(pos_ref, f_ref, x_ref, z_ref, c_ref, cz_ref, out_ref):
    core1, odd = pos_ref[0] == 1, pos_ref[1] == 1
    two = jnp.where(odd, f_ref[0], f_ref[4])
    far = jnp.where(odd, f_ref[4], f_ref[0])
    side = jnp.where(core1, f_ref[1], f_ref[3])
    own_side = core1 == odd
    fc = jnp.where(own_side, side, 0.0)
    fz = jnp.where(own_side, 0.0, side)
    weighted((two, far, fc, fz), (x_ref, z_ref, c_ref, cz_ref), out_ref)


def core_partial_kernel(pos_ref, f_ref, x_ref, y_ref, z_ref, out_ref):
    core1, odd = pos_ref[0] == 1, pos_ref[1] == 1
    near = jnp.where(core1, f_ref[1], f_ref[3])
    far = jnp.where(core1, f_ref[3], f_ref[1])
    by_pair = core1 == odd
    weighted((near, jnp.where(by_pair, far, 0.0), jnp.where(by_pair, 0.0, far)), (x_ref, y_ref, z_ref), out_ref)


def greater_window_kernel(pos_ref, f_ref, x_ref, c_ref, r_ref, out_ref):
    core1 = pos_ref[0] == 1
    weighted((f_ref[2], jnp.where(core1, f_ref[3], f_ref[1]), None), (x_ref, c_ref, r_ref), out_ref)


def lesser_window_kernel(pos_ref, f_ref, x_ref, y_ref, z_ref, r_ref, out_ref):
    odd = pos_ref[1] == 1
    fy = jnp.where(odd, f_ref[4], f_ref[0])
    fz = jnp.where(odd, f_ref[0], f_ref[4])
    weighted((f_ref[2], fy, fz, None), (x_ref, y_ref, z_ref, r_ref), out_ref)


def combine(kernel, pos, factors, *blocks):
    return pl.pallas_call(
        kernel,
        out_shape=jax.ShapeDtypeStruct(SHAPE, BF16),
        in_specs=[SMEM, SMEM] + [VMEM] * len(blocks),
        out_specs=VMEM,
        compiler_params=PARAMS,
        cost_estimate=pl.CostEstimate(flops=2**21, bytes_accessed=2**21, transcendentals=0),
    )(pos, factors, *blocks)


def stage_kernel(a_ref, b_ref, c_ref, d_ref):
    c_ref[...] = a_ref[...]
    d_ref[...] = b_ref[...]


def stage(a, b):
    shapes = [jax.ShapeDtypeStruct(v.shape, BF16) for v in (a, b)]
    return pl.pallas_call(
        stage_kernel, out_shape=shapes, in_specs=[VMEM, VMEM], out_specs=[VMEM, VMEM], compiler_params=PARAMS
    )(a, b)


def sigma_part(occ_ref, off_ref, own_ref, below_ref, above_ref, mat_ref, e, cols, plus_up):
    acc = None
    for branch in range(BRANCHES):
        n = occ_ref[branch]
        one = off_ref[branch] == 1
        up_factor = n + 1.0 if plus_up else n
        down_factor = n if plus_up else n + 1.0
        if e == 0:
            upper = jnp.where(one, own_ref[1, :, cols], above_ref[0, :, cols])
            lower = jnp.where(one, below_ref[1, :, cols], below_ref[0, :, cols])
        else:
            upper = jnp.where(one, above_ref[0, :, cols], above_ref[1, :, cols])
            lower = jnp.where(one, own_ref[0, :, cols], below_ref[1, :, cols])
        mixed = (up_factor * upper.astype(F32) + down_factor * lower.astype(F32)).astype(BF16)
        left = jnp.dot(mat_ref[branch], mixed, preferred_element_type=F32).astype(BF16)
        right = lax.dot_general(left, mat_ref[branch], (((1,), (1,)), ((), ())), preferred_element_type=F32)
        acc = right if acc is None else acc + right
    return acc.astype(BF16)


def by_parity(pos_ref, a_ref, b_ref, body):
    swap = pos_ref[2] == 1
    pl.when(swap)(lambda: body(b_ref, a_ref))
    pl.when(jnp.logical_not(swap))(lambda: body(a_ref, b_ref))


def sigma_kernel(pos_ref, occ_ref, off_ref, own_ref, b_ref, a_ref, mat_ref, out_ref, *, plus_up):
    def body(below_ref, above_ref):
        for e in range(2):
            for h in range(2):
                cols = slice(h * ORB, (h + 1) * ORB)
                out_ref[e, :, cols] = sigma_part(
                    occ_ref, off_ref, own_ref, below_ref, above_ref, mat_ref, e, cols, plus_up
                )

    by_parity(pos_ref, a_ref, b_ref, body)


def sigma(plus_up, pos, occupation, offsets, *blocks):
    return pl.pallas_call(
        functools.partial(sigma_kernel, plus_up=plus_up),
        out_shape=jax.ShapeDtypeStruct(SHAPE, BF16),
        in_specs=[SMEM] * 3 + [VMEM] * len(blocks),
        out_specs=VMEM,
        compiler_params=PARAMS,
        cost_estimate=pl.CostEstimate(flops=2**30, bytes_accessed=3 * 2**20, transcendentals=0),
    )(pos, occupation, offsets, *blocks)


def local(lesser, greater, coupling, occupation, offsets, readers, weights):
    count = lax.axis_size("kz")
    energies = lax.axis_size("en")
    k = lax.axis_index("kz")
    pos = jnp.stack((k & 1, (k >> 1) & 1, lax.axis_index("en") & 1)).astype(jnp.int32)

    def kz(block, route):
        return lax.ppermute(block, "kz", route)

    xl = lesser.reshape(SHAPE)
    xg = greater.reshape(SHAPE)
    mats = coupling[0]
    xgv, mats = stage(xg, mats)
    f = weights * readers[0].astype(F32)

    yl = kz(xl, swap_route(count, 2))
    zg = kz(xg, plane_route(count, -1))
    cg = kz(xg, swap_route(count, 1))
    fy = kz(f, swap_route(count, 2))
    yl, f, fy, pos, xgv, mats = lax.optimization_barrier((yl, f, fy, pos, xgv, mats))
    zl = kz(yl, plane_route(count, 1))
    czg = kz(zg, swap_route(count, 1))
    pg = combine(pair_partial_kernel, pos, fy, xgv, zg, cg, czg)
    rg = kz(pg, swap_route(count, 2))
    late, _ = lax.optimization_barrier((f, pg))
    fc = kz(late, swap_route(count, 1))
    zl, fc = lax.optimization_barrier((zl, fc))
    ql = combine(core_partial_kernel, pos, fc, xl, yl, zl)
    rl = kz(ql, swap_route(count, 1))
    wg = combine(greater_window_kernel, pos, f, xgv, cg, rg)
    wl = combine(lesser_window_kernel, pos, f, xl, yl, zl, rl)

    odd_pairs, even_pairs = pair_route(energies, 1), pair_route(energies, 0)
    bl = lax.ppermute(wl, "en", even_pairs)
    al = lax.ppermute(wl, "en", odd_pairs)
    bg = lax.ppermute(wg, "en", even_pairs)
    ag = lax.ppermute(wg, "en", odd_pairs)
    sl = sigma(True, pos, occupation, offsets, wl, bl, al, mats)
    sg = sigma(False, pos, occupation, offsets, wg, bg, ag, mats)
    return sl.reshape(lesser.shape), sg.reshape(greater.shape)


def solution(mesh):
    wide = P("kz", "en", None, None, None)
    return jax.shard_map(
        local,
        mesh=mesh,
        in_specs=(wide, wide, P(), P(), P(), P("kz", None), P()),
        out_specs=(wide, wide),
        check_vma=False,
    )
```
